128 devices in a mesh: rows: 8 (over y, x_hi), cols: 16 (over x_lo, z, core).
Axes of the slice: x: 4 (x_hi: 2, x_lo: 2; x = x_hi * 2 + x_lo), y: 4, z: 4, core: 2. Of those that a mesh axis runs over, the one named last changes fastest.
Arguments:
- incident: float32 [2, 1024, 4096], P(None, None, ('rows', 'cols')), may hold values from -6 to 6
- diag_first: float32 [4096, 4096], P('rows', 'cols'), may hold values from -1 to 2, as said below
- coupling: float32 [4096, 4096], P('rows', 'cols'), may hold values from -0.09375 to 0.09375
- diag_second: float32 [4096, 4096], P('rows', 'cols'), may hold values from -1 to 2, as said below
- trail_first: float32 [20480, 4096], P('rows', 'cols'), may hold values from -0.09375 to 0.09375
- trail_second: float32 [20480, 4096], P('rows', 'cols'), may hold values from -0.09375 to 0.09375
- trail_rhs: float32 [1024, 20480], P('cols', 'rows'), may hold values from -6 to 6
Outputs:
- solved: float32 [2, 1024, 4096], P(None, 'cols', 'rows')
- updated: float32 [1024, 20480], P('cols', 'rows')
The draws below stay inside these ranges and needn't reach their ends.
Inputs may be any that keep to these rules, and one draw needn't show every extreme that they name: `diag_first`: lower triangular: zero above the diagonal, diagonal entries between 0.8 and 1.25. `diag_second`: lower triangular: zero above the diagonal, diagonal entries between 0.8 and 1.25.
All inputs are finite; a program needn't handle non-finite values.
Results may differ from the reference program's by a relative error of at most 0.00011.
Values sent between devices are 32-bit elements; how exact they have to be, the bound alone decides.
A program may use at most 128 MiB of HBM per device.

```python
import jax
import jax.numpy as jnp
from jax import lax

NB = 4096
TRAIL = 20480
H = 1024


def lower_block(noise, diag_key):
    row_ids = lax.broadcasted_iota(jnp.int32, (NB, NB), 0)
    column_ids = lax.broadcasted_iota(jnp.int32, (NB, NB), 1)
    diagonal = 0.8 + 0.45 * jax.random.uniform(diag_key, (NB, 1), jnp.float32)
    below = jnp.where(column_ids < row_ids, noise * (0.8 / NB ** 0.5), 0.0)
    return jnp.where(column_ids == row_ids, diagonal, below).astype(jnp.float32)


def draw_diag_first(key, part):
    key = jax.random.fold_in(key, 11)
    noise_key, diag_key = jax.random.split(key)
    noise = jnp.clip(jax.random.normal(noise_key, (NB, NB), jnp.float32), -5.0, 5.0)
    return lower_block(noise, diag_key)


def draw_diag_second(key, part):
    key = jax.random.fold_in(key, 23)
    noise_key, diag_key = jax.random.split(key)
    noise = jnp.clip(jax.random.normal(noise_key, (NB, NB), jnp.float32), -5.0, 5.0)
    return lower_block(noise, diag_key)


def steps_of(key, dims, shards, smallest, top_value):
    level = 1.0
    for dim, parts in shards:
        heights = jax.random.uniform(jax.random.fold_in(jax.random.fold_in(key, 6), dim), (parts,), jnp.float32, smallest / len(shards), top_value / len(shards))
        level = level * jnp.repeat(jnp.exp(heights), dims[dim] // parts).reshape((-1,) + (1,) * (len(dims) - 1 - dim))
    return level


def normal_values(stream_key, extent, spread, most, pieces=(), dtype=jnp.bfloat16):
    drawn = jax.random.normal(stream_key, extent, jnp.float32) * spread
    if len(pieces) > 0:
        drawn = steps_of(stream_key, extent, pieces, -0.22, 0.18) * drawn
    return jnp.clip(drawn, min=-most, max=most).astype(dtype)


def setup_inputs(seed: int = 0) -> dict:
    key_of = jax.random.split(jax.random.key(seed), 8)
    incident = normal_values(key_of[0], (2, H, NB), 1.0, 6.0, ((2, 128),), jnp.float32)
    diag_first = draw_diag_first(jax.random.fold_in(key_of[7], 71), 0)
    coupling = normal_values(key_of[2], (NB, NB), NB ** -0.5, 0.09375, ((0, 8), (1, 16)), jnp.float32)
    diag_second = draw_diag_second(jax.random.fold_in(key_of[7], 71), 0)
    trail_first = normal_values(key_of[4], (TRAIL, NB), NB ** -0.5, 0.09375, ((0, 8), (1, 16)), jnp.float32)
    trail_second = normal_values(key_of[5], (TRAIL, NB), NB ** -0.5, 0.09375, ((0, 8), (1, 16)), jnp.float32)
    trail_rhs = normal_values(key_of[6], (H, TRAIL), 1.0, 6.0, ((0, 16), (1, 8)), jnp.float32)
    return dict(incident=incident, diag_first=diag_first, coupling=coupling, diag_second=diag_second, trail_first=trail_first, trail_second=trail_second, trail_rhs=trail_rhs)


def product_rows(left, right):
    return lax.dot_general(left, right, (((1,), (1,)), ((), ())), precision=lax.Precision.HIGHEST, preferred_element_type=jnp.float32)


def reference(incident, diag_first, coupling, diag_second, trail_first, trail_second, trail_rhs):
    solved_first = product_rows(incident[0], diag_first)
    reduced = incident[1] - product_rows(solved_first, coupling)
    solved_second = product_rows(reduced, diag_second)
    solved = jnp.stack([solved_first, solved_second])
    updated = trail_rhs - (product_rows(solved_first, trail_first) + product_rows(solved_second, trail_second))
    return solved, updated
```

```python
import functools

import jax
import jax.numpy as jnp
from jax import lax
from jax.experimental import pallas as pl
from jax.experimental.pallas import tpu as pltpu
from jax.sharding import PartitionSpec as P

MESH = pl.DeviceIdType.MESH
BF = jnp.bfloat16
F32 = jnp.float32

G = 2
HG = 64 // G
HP = HG // 4
W = 512
TR = 2560
PC = 512
X_FIRST = (0, 1, 2)
Z_FIRST = (3, 4)
SEND_ORDER = (3, 0, 1, 4, 2)


def split(x):
    hi = x.astype(BF)
    return hi, (x - hi.astype(F32)).astype(BF)


def product3(left, right_hi, right_lo):
    hi, lo = split(left)

    def dot(a, b):
        return lax.dot_general(a, b, (((1,), (1,)), ((), ())), preferred_element_type=F32)

    return dot(hi, right_hi) + (dot(hi, right_lo) + dot(lo, right_hi))


def kernel(
    x_ref, d1_ref, c_ref, d2_ref, t1_ref, t2_ref, rhs_ref,
    solved_ref, updated_ref,
    own_s, sib_s, own_t, sib_t, rhs,
    wh, wl, th, tl,
    xr, xt, xs, x1b, x1s,
    part, got, summed, sol,
    upd, xa, za, zb, xb,
    loc, sib_tx, sib_rx, x_tx, x_rx, st_tx, st_rx, u_tx, u_rx,
):
    r = lax.axis_index("rows")
    c = lax.axis_index("cols")
    y, xh = r // 2, r % 2
    q, k = c // 2, c % 2
    xl, z = q // 4, q % 4
    own_lanes = pl.ds(pl.multiple_of(k * 256, 256), 256)
    sib_lanes = pl.ds(pl.multiple_of((1 - k) * 256, 256), 256)
    sibling = (r, q * 2 + (1 - k))
    diagonal = r == q

    def send(src, dst, tx, rx, dev):
        pltpu.make_async_remote_copy(
            src_ref=src, dst_ref=dst, send_sem=tx, recv_sem=rx, device_id=dev, device_id_type=MESH
        ).start()

    def settle(ref, sem):
        pltpu.make_async_copy(ref, ref, sem).wait()

    own = [(d1_ref, own_s.at[0]), (c_ref, own_s.at[1]), (d2_ref, own_s.at[2]),
           (t1_ref, own_t.at[0]), (t2_ref, own_t.at[1]), (rhs_ref, rhs)]
    loads = [pltpu.make_async_copy(src, dst, loc.at[i]) for i, (src, dst) in enumerate(own)]
    for load in loads:
        load.start()

    barrier = pltpu.get_barrier_semaphore()
    plane = [(dq, dk) for dq in range(8) for dk in range(2) if (dq, dk) != (0, 0)]

    def plane_dev(dq, dk):
        return (r, ((q + dq) % 8) * 2 + (k + dk) % 2)

    def y_dev(d):
        return (((y + d) % 4) * 2 + xh, c)

    def greet(dev):
        pl.semaphore_signal(barrier, inc=1, device_id=dev, device_id_type=MESH)

    for dq, dk in plane:
        greet(plane_dev(dq, dk))
    for d in (1, 2, 3):
        greet(y_dev(d))
    for j in range(8):
        greet((q, j * 2 + (1 - k)))

        @pl.when(jnp.logical_not(jnp.logical_and(diagonal, j == q)))
        def _():
            greet((q, j * 2 + k))

    low = lax.broadcasted_iota(jnp.int32, (32, 128), 1) < 64
    for t in range(4):
        a = x_ref[0, :, 256 * t : 256 * t + 128]
        b = x_ref[0, :, 256 * t + 128 : 256 * t + 256]
        xr[0, :, 128 * t : 128 * t + 128] = jnp.where(low, a, pltpu.roll(b, 64, 1))
        xr[1, :, 128 * t : 128 * t + 128] = jnp.where(low, pltpu.roll(a, 64, 1), b)

    pl.semaphore_wait(barrier, 33 + jnp.where(diagonal, 0, 1))

    for dk in range(2):
        kk = (k + dk) % 2
        for jy in range(4):
            rows = pl.ds(jy * 8, 8)
            for jx in range(2):
                j = jy * 2 + jx
                src, dst = xr.at[kk, rows], xt.at[c, rows]
                if dk == 1:
                    send(src, dst, x_tx.at[0], x_rx.at[0], (j, r * 2 + kk))
                else:
                    me = jnp.logical_and(diagonal, r == j)

                    @pl.when(jnp.logical_not(me))
                    def _():
                        send(src, dst, x_tx.at[0], x_rx.at[0], (j, r * 2 + kk))

                    @pl.when(me)
                    def _():
                        pltpu.make_async_copy(src, dst, x_rx.at[0]).start()

    small = [d1_ref, c_ref, d2_ref]
    send(small[0], sib_s.at[0], sib_tx.at[0], sib_rx.at[0], sibling)
    for dq, dk in plane:
        lanes = pl.ds(pl.multiple_of(((q + dq) % 8) * 128, 128), 128)
        send(x_ref.at[1, :, lanes], x1b.at[c], x_tx.at[2], x_rx.at[2], plane_dev(dq, dk))
    for i in (1, 2):
        send(small[i], sib_s.at[i], sib_tx.at[i], sib_rx.at[i], sibling)
    for i, t_ref in enumerate((t1_ref, t2_ref)):
        send(t_ref, sib_t.at[i], sib_tx.at[3 + i], sib_rx.at[3 + i], sibling)
    x1b[c] = x_ref[1, :, pl.ds(pl.multiple_of(q * 128, 128), 128)]

    def ready_small(i):
        loads[i].wait()
        wh[i, :, own_lanes], wl[i, :, own_lanes] = split(own_s[i])
        settle(sib_s.at[i], sib_rx.at[i])
        wh[i, :, sib_lanes], wl[i, :, sib_lanes] = split(sib_s[i])

    def ready_trail(i):
        loads[3 + i].wait()
        settle(sib_t.at[i], sib_rx.at[3 + i])

        @pl.loop(0, 20)
        def _(n):
            rows = pl.ds(pl.multiple_of(n * 128, 128), 128)
            th[i, rows, own_lanes], tl[i, rows, own_lanes] = split(own_t[i, rows, :])
            th[i, rows, sib_lanes], tl[i, rows, sib_lanes] = split(sib_t[i, rows, :])

    ready_small(0)
    mine = pl.ds(pl.multiple_of(y * 8, 8), 8)
    settle(xt.at[:, mine], x_rx.at[0])
    for d in (1, 2, 3):
        send(xt.at[:, mine], xt.at[:, mine], x_tx.at[1], x_rx.at[1], y_dev(d))
    ready_small(1)
    ready_small(2)
    settle(xt.at[:, pl.ds(0, 24)], x_rx.at[1])
    for n in range(4):
        block = xt[:, :, 128 * n : 128 * n + 128].reshape(512, 128)
        xs[2 * n : 2 * n + 2] = block.T.reshape(2, 64, W)

    def multiply(s, g):
        if s == 0:
            left = xs[:, g * HG : (g + 1) * HG, :]
        else:
            settle(sol.at[s - 1, g, :, pl.ds(0, 3 * HP)], st_rx.at[2, s - 1, g])
            left = sol[s - 1, g]
        out = product3(left.reshape(8 * HG, W), wh[s], wl[s])
        part[s, g] = out.reshape(8, HG, W)
        for d in range(1, 8):
            to = (q + d) % 8
            send(part.at[s, g, to], got.at[s, g, d - 1], st_tx.at[0, s, g], st_rx.at[0, s, g], (r, to * 2 + k))

    def sum_up(s, g):
        settle(got.at[s, g], st_rx.at[0, s, g])
        total = part[s, g, q]
        for d in range(7):
            total = total + got[s, g, d]
        rows = slice(g * HG, (g + 1) * HG)
        if s == 1:
            total = x1s[k, rows] - total
        else:
            solved_ref[s // 2, rows] = total
        summed[s, g] = total
        for jy in range(4):
            piece = pl.ds(jy * HP, HP)
            for jx in range(2):
                j = jy * 2 + jx
                src, dst = summed.at[s, g, piece], sol.at[s, g, q, piece]
                me = jnp.logical_and(diagonal, r == j)

                @pl.when(jnp.logical_not(me))
                def _():
                    send(src, dst, st_tx.at[1, s, g], st_rx.at[1, s, g], (j, r * 2 + k))

                @pl.when(me)
                def _():
                    pltpu.make_async_copy(src, dst, st_rx.at[1, s, g]).start()

    def spread(s, g):
        piece = pl.ds(pl.multiple_of(y * HP, HP), HP)
        settle(sol.at[s, g, :, piece], st_rx.at[1, s, g])
        for d in (1, 2, 3):
            block = sol.at[s, g, :, piece]
            send(block, block, st_tx.at[2, s, g], st_rx.at[2, s, g], y_dev(d))

    groups = range(G)
    for g in groups:
        multiply(0, g)
    ready_trail(0)
    ready_trail(1)
    for g in groups:
        sum_up(0, g)
    for g in groups:
        spread(0, g)
    settle(x1b.at[pl.ds(0, 15)], x_rx.at[2])
    x1s[...] = x1b[...].reshape(512, 128).T.reshape(2, 64, W)
    for g in groups:
        multiply(1, g)
    for g in groups:
        for p in range(5):
            columns = slice(p * PC, (p + 1) * PC)
            left = sol[0, g].reshape(8 * HG, W)
            upd[g, :, :, columns] = product3(left, th[0, columns], tl[0, columns]).reshape(8, HG, PC)
    for g in groups:
        sum_up(1, g)
    for g in groups:
        spread(1, g)
    for g in groups:
        multiply(2, g)
    for g in groups:
        sum_up(2, g)
    for g in groups:
        spread(2, g)

    across = (r, ((1 - xl) * 4 + z) * 2 + k)

    def z_dev(d):
        return (r, (xl * 4 + (z + d) % 4) * 2 + k)

    for g in groups:
        settle(sol.at[2, g, :, pl.ds(0, 3 * HP)], st_rx.at[2, 2, g])
        for p in SEND_ORDER:
            columns = slice(p * PC, (p + 1) * PC)
            left = sol[2, g].reshape(8 * HG, W)
            upd[g, :, :, columns] += product3(left, th[1, columns], tl[1, columns]).reshape(8, HG, PC)
            lanes = pl.ds(p * PC, PC)
            if p in X_FIRST:
                send(upd.at[g, pl.ds((1 - xl) * 4, 4), :, lanes], xa.at[g, p], u_tx.at[0, g, p], u_rx.at[0, g, p], across)
            else:
                for d in (1, 2, 3):
                    zz = (z + d) % 4
                    for x in range(2):
                        send(upd.at[g, x * 4 + zz, :, lanes], zb.at[g, p - 3, d - 1, x],
                             u_tx.at[0, g, p], u_rx.at[0, g, p], z_dev(d))
    for g in groups:
        for p in SEND_ORDER:
            columns = slice(p * PC, (p + 1) * PC)
            lanes = pl.ds(p * PC, PC)
            if p in X_FIRST:
                settle(xa.at[g, p], u_rx.at[0, g, p])
                upd[g, pl.ds(xl * 4, 4), :, columns] += xa[g, p]
                for d in (1, 2, 3):
                    send(upd.at[g, xl * 4 + (z + d) % 4, :, lanes], za.at[g, p, d - 1],
                         u_tx.at[1, g, p], u_rx.at[1, g, p], z_dev(d))
            else:
                settle(zb.at[g, p - 3], u_rx.at[0, g, p])
                for x in range(2):
                    terms = (zb[g, p - 3, 0, x] + zb[g, p - 3, 1, x]) + zb[g, p - 3, 2, x]
                    upd[g, x * 4 + z, :, columns] += terms
                send(upd.at[g, (1 - xl) * 4 + z, :, lanes], xb.at[g, p - 3], u_tx.at[1, g, p], u_rx.at[1, g, p], across)
    loads[5].wait()
    for g in groups:
        rows = slice(g * HG, (g + 1) * HG)
        for p in SEND_ORDER:
            columns = slice(p * PC, (p + 1) * PC)
            mine = upd[g, q, :, columns]
            if p in X_FIRST:
                settle(za.at[g, p], u_rx.at[1, g, p])
                mine = mine + ((za[g, p, 0] + za[g, p, 1]) + za[g, p, 2])
            else:
                settle(xb.at[g, p - 3], u_rx.at[1, g, p])
                mine = mine + xb[g, p - 3]
            updated_ref[rows, columns] = rhs[rows, columns] - mine

    for i in range(3):
        settle(sib_s.at[i], sib_tx.at[i])
    for i in range(2):
        settle(sib_t.at[i], sib_tx.at[3 + i])

    @pl.when(diagonal)
    def _():
        settle(xt.at[pl.ds(0, 15), pl.ds(0, 8)], x_tx.at[0])

    @pl.when(jnp.logical_not(diagonal))
    def _():
        settle(xt.at[:, pl.ds(0, 8)], x_tx.at[0])

    settle(xt.at[:, pl.ds(0, 24)], x_tx.at[1])
    settle(x1b.at[pl.ds(0, 15)], x_tx.at[2])
    for s in range(3):
        for g in groups:
            settle(got.at[s, g], st_tx.at[0, s, g])

            @pl.when(diagonal)
            def _():
                settle(sol.at[s, g, pl.ds(0, 7), pl.ds(0, HP)], st_tx.at[1, s, g])

            @pl.when(jnp.logical_not(diagonal))
            def _():
                settle(sol.at[s, g, :, pl.ds(0, HP)], st_tx.at[1, s, g])

            settle(sol.at[s, g, :, pl.ds(0, 3 * HP)], st_tx.at[2, s, g])
    for g in groups:
        for p in range(5):
            if p in X_FIRST:
                settle(xa.at[g, p], u_tx.at[0, g, p])
                settle(za.at[g, p], u_tx.at[1, g, p])
            else:
                settle(zb.at[g, p - 3], u_tx.at[0, g, p])
                settle(xb.at[g, p - 3], u_tx.at[1, g, p])


def on_device(incident, diag_first, coupling, diag_second, trail_first, trail_second, trail_rhs):
    whole = pl.BlockSpec(memory_space=pltpu.VMEM)
    far = pl.BlockSpec(memory_space=pl.ANY)
    dma = pltpu.SemaphoreType.DMA
    return pl.pallas_call(
        kernel,
        out_shape=(jax.ShapeDtypeStruct((2, 64, W), F32), jax.ShapeDtypeStruct((64, TR), F32)),
        in_specs=[whole] + [far] * 6,
        out_specs=(whole, whole),
        scratch_shapes=[
            pltpu.VMEM((3, W, 256), F32),
            pltpu.VMEM((3, W, 256), F32),
            pltpu.VMEM((2, TR, 256), F32),
            pltpu.VMEM((2, TR, 256), F32),
            pltpu.VMEM((64, TR), F32),
            pltpu.VMEM((3, W, W), BF),
            pltpu.VMEM((3, W, W), BF),
            pltpu.VMEM((2, TR, W), BF),
            pltpu.VMEM((2, TR, W), BF),
            pltpu.VMEM((2, 32, 512), F32),
            pltpu.VMEM((16, 32, 512), F32),
            pltpu.VMEM((8, 64, W), F32),
            pltpu.VMEM((16, 32, 128), F32),
            pltpu.VMEM((2, 64, W), F32),
            pltpu.VMEM((3, G, 8, HG, W), F32),
            pltpu.VMEM((3, G, 7, HG, W), F32),
            pltpu.VMEM((3, G, HG, W), F32),
            pltpu.VMEM((3, G, 8, HG, W), F32),
            pltpu.VMEM((G, 8, HG, TR), F32),
            pltpu.VMEM((G, len(X_FIRST), 4, HG, PC), F32),
            pltpu.VMEM((G, len(X_FIRST), 3, HG, PC), F32),
            pltpu.VMEM((G, len(Z_FIRST), 3, 2, HG, PC), F32),
            pltpu.VMEM((G, len(Z_FIRST), HG, PC), F32),
            dma((6,)), dma((5,)), dma((5,)), dma((3,)), dma((3,)),
            dma((3, 3, G)), dma((3, 3, G)), dma((2, G, 5)), dma((2, G, 5)),
        ],
        compiler_params=pltpu.CompilerParams(
            collective_id=0, has_side_effects=True, vmem_limit_bytes=60 * 1024 * 1024
        ),
        name="solve",
    )(jnp.swapaxes(incident, 1, 2), diag_first, coupling, diag_second, trail_first, trail_second, trail_rhs)


def solution(mesh):
    split_all = P("rows", "cols")
    return jax.shard_map(
        on_device,
        mesh=mesh,
        in_specs=(P(None, None, ("rows", "cols")),) + (split_all,) * 5 + (P("cols", "rows"),),
        out_specs=(P(None, "cols", "rows"), P("cols", "rows")),
        check_vma=False,
    )
```

```python
import functools

import jax
import jax.numpy as jnp
from jax import lax
from jax.experimental import pallas as pl
from jax.experimental.pallas import tpu as pltpu
from jax.sharding import PartitionSpec as P

MESH = pl.DeviceIdType.MESH
BF = jnp.bfloat16
F32 = jnp.float32

G = 4
HG = 64 // G
W = 512
HL = 512 // G
TR = 2560
PIECES = ((1536, 512, 0), (0, 768, 1), (768, 768, 1), (2048, 512, 0))
XW, ZW = 768, 512
STEP = 4


def split(x):
    hi = x.astype(BF)
    return hi, (x - hi.astype(F32)).astype(BF)


def product3(left, right_hi, right_lo):
    hi, lo = split(left)

    def dot(a, b):
        return lax.dot_general(a, b, (((1,), (1,)), ((), ())), preferred_element_type=F32)

    return dot(hi, right_hi) + (dot(hi, right_lo) + dot(lo, right_hi))


def kernel(
    x_ref, d1_ref, c_ref, d2_ref, t1_ref, t2_ref, rhs_ref,
    solved_ref, updated_ref,
    own_s, sib_s, own_t, sib_t, rhs,
    wh, wl, th, tl,
    xr, xt, x1b, x1s,
    part, got, summed, sol,
    upd, xa, za, zb, xb,
    loc, sib_tx, sib_rx, x_tx, x_rx, xg_tx, xg_rx, st_tx, st_rx, u_tx, u_rx,
):
    r = lax.axis_index("rows")
    c = lax.axis_index("cols")
    y, xh = r // 2, r % 2
    q, k = c // 2, c % 2
    xl, z = q // 4, q % 4
    own_lanes = pl.ds(pl.multiple_of(k * 256, 256), 256)
    sib_lanes = pl.ds(pl.multiple_of((1 - k) * 256, 256), 256)
    sibling = (r, q * 2 + (1 - k))
    diagonal = r == q

    def send(src, dst, tx, rx, dev):
        pltpu.make_async_remote_copy(
            src_ref=src, dst_ref=dst, send_sem=tx, recv_sem=rx, device_id=dev, device_id_type=MESH
        ).start()

    def settle(ref, sem):
        pltpu.make_async_copy(ref, ref, sem).wait()

    own = [(d1_ref, own_s.at[0]), (c_ref, own_s.at[1]), (d2_ref, own_s.at[2]),
           (t1_ref, own_t.at[0]), (t2_ref, own_t.at[1]), (rhs_ref, rhs)]
    loads = [pltpu.make_async_copy(src, dst, loc.at[i]) for i, (src, dst) in enumerate(own)]
    for load in loads:
        load.start()

    barrier = pltpu.get_barrier_semaphore()
    plane = [(dq, dk) for dq in range(8) for dk in range(2) if (dq, dk) != (0, 0)]

    def plane_dev(dq, dk):
        return (r, ((q + dq) % 8) * 2 + (k + dk) % 2)

    def y_dev(d):
        return (((y + d) % 4) * 2 + xh, c)

    def greet(dev):
        pl.semaphore_signal(barrier, inc=1, device_id=dev, device_id_type=MESH)

    for dq, dk in plane:
        greet(plane_dev(dq, dk))
    for d in (1, 2, 3):
        greet(y_dev(d))
    for j in range(8):
        greet((q, j * 2 + (1 - k)))

        @pl.when(jnp.logical_not(jnp.logical_and(diagonal, j == q)))
        def _():
            greet((q, j * 2 + k))

    per = 128 // HG
    place = lax.broadcasted_iota(jnp.int32, (32, 128), 1) // HG
    for core in range(2):
        for t in range(4):
            tile = None
            for j in range(per):
                chip = (t * per + j) % 8
                here = core * G + (t * per + j) // 8
                taken = x_ref[0, :, chip * 128 : chip * 128 + 128]
                shift = ((j - here) * HG) % 128
                if shift:
                    taken = pltpu.roll(taken, shift, 1)
                tile = taken if tile is None else jnp.where(place == j, taken, tile)
            xr[core, :, t * 128 : t * 128 + 128] = tile

    pl.semaphore_wait(barrier, 33 + jnp.where(diagonal, 0, 1))

    for dk in range(2):
        kk = (k + dk) % 2
        for jy in range(4):
            rows = pl.ds(jy * 8, 8)
            for jx in range(2):
                j = jy * 2 + jx
                src, dst = xr.at[kk, rows], xt.at[c, rows]
                if dk == 1:
                    send(src, dst, x_tx.at[0], x_rx.at[0], (j, r * 2 + kk))
                else:
                    me = jnp.logical_and(diagonal, r == j)

                    @pl.when(jnp.logical_not(me))
                    def _():
                        send(src, dst, x_tx.at[0], x_rx.at[0], (j, r * 2 + kk))

                    @pl.when(me)
                    def _():
                        pltpu.make_async_copy(src, dst, x_rx.at[0]).start()

    small = [d1_ref, c_ref, d2_ref]
    send(small[0], sib_s.at[0], sib_tx.at[0], sib_rx.at[0], sibling)

    def ready_small(i):
        loads[i].wait()
        wh[i, :, own_lanes], wl[i, :, own_lanes] = split(own_s[i])
        settle(sib_s.at[i], sib_rx.at[i])
        wh[i, :, sib_lanes], wl[i, :, sib_lanes] = split(sib_s[i])

    def ready_trail(i):
        loads[3 + i].wait()
        settle(sib_t.at[i], sib_rx.at[3 + i])

        @pl.loop(0, 20)
        def _(n):
            rows = pl.ds(pl.multiple_of(n * 128, 128), 128)
            th[i, rows, own_lanes], tl[i, rows, own_lanes] = split(own_t[i, rows, :])
            th[i, rows, sib_lanes], tl[i, rows, sib_lanes] = split(sib_t[i, rows, :])

    ready_small(0)
    mine = pl.ds(pl.multiple_of(y * 8, 8), 8)
    settle(xt.at[:, mine], x_rx.at[0])
    for g in range(G):
        for d in (1, 2, 3):
            block = xt.at[:, mine, pl.ds(g * HL, HL)]
            send(block, block, xg_tx.at[g], xg_rx.at[g], y_dev(d))
    send(small[1], sib_s.at[1], sib_tx.at[1], sib_rx.at[1], sibling)
    for dq, dk in plane:
        lanes = pl.ds(pl.multiple_of(((q + dq) % 8) * 128, 128), 128)
        send(x_ref.at[1, :, lanes], x1b.at[c], x_tx.at[1], x_rx.at[1], plane_dev(dq, dk))
    x1b[c] = x_ref[1, :, pl.ds(pl.multiple_of(q * 128, 128), 128)]
    send(small[2], sib_s.at[2], sib_tx.at[2], sib_rx.at[2], sibling)
    for i, t_ref in enumerate((t1_ref, t2_ref)):
        send(t_ref, sib_t.at[i], sib_tx.at[3 + i], sib_rx.at[3 + i], sibling)

    def three_lanes(s, g):
        return sol.at[s, g, :, :, pl.ds(0, 384)]

    def own_piece():
        return pl.ds(pl.multiple_of(y * 128, 128), 128)

    def multiply(s, g):
        if s == 0:
            settle(xt.at[:, pl.ds(0, 24), pl.ds(0, HL)], xg_rx.at[g])
            left = xt[:, :, g * HL : (g + 1) * HL].reshape(W, HL).T
        else:
            settle(three_lanes(s - 1, g), st_rx.at[2, s - 1, g])
            left = sol[s - 1, g].reshape(8 * HG, W)
        out = product3(left, wh[s], wl[s])
        part[s, g] = out.reshape(8, HG, W)
        for d in range(1, 8):
            to = (q + d) % 8
            send(part.at[s, g, to], got.at[s, g, d - 1], st_tx.at[0, s, g], st_rx.at[0, s, g], (r, to * 2 + k))

    def sum_up(s, g):
        settle(got.at[s, g], st_rx.at[0, s, g])
        total = part[s, g, q]
        for d in range(7):
            total = total + got[s, g, d]
        rows = slice(g * HG, (g + 1) * HG)
        if s == 1:
            total = x1s[k, rows] - total
        else:
            solved_ref[s // 2, rows] = total
        summed[s, g] = total
        for jy in range(4):
            piece = pl.ds(jy * 128, 128)
            for jx in range(2):
                j = jy * 2 + jx
                src, dst = summed.at[s, g, :, piece], sol.at[s, g, q, :, piece]
                me = jnp.logical_and(diagonal, r == j)

                @pl.when(jnp.logical_not(me))
                def _():
                    send(src, dst, st_tx.at[1, s, g], st_rx.at[1, s, g], (j, r * 2 + k))

                @pl.when(me)
                def _():
                    pltpu.make_async_copy(src, dst, st_rx.at[1, s, g]).start()

    def spread(s, g):
        block = sol.at[s, g, :, :, own_piece()]
        settle(block, st_rx.at[1, s, g])
        for d in (1, 2, 3):
            send(block, block, st_tx.at[2, s, g], st_rx.at[2, s, g], y_dev(d))

    def ready_second():
        settle(x1b.at[pl.ds(0, 15)], x_rx.at[1])
        x1s[...] = x1b[...].reshape(512, 128).T.reshape(2, 64, W)

    def first_trail(p):
        start, width, _ = PIECES[p]
        columns = slice(start, start + width)
        left = sol[0].reshape(512, W)
        upd[:, :, :, columns] = product3(left, th[0, columns], tl[0, columns]).reshape(G, 8, HG, width)

    across = (r, ((1 - xl) * 4 + z) * 2 + k)

    def z_dev(d):
        return (r, (xl * 4 + (z + d) % 4) * 2 + k)

    def second_trail(g):
        settle(three_lanes(2, g), st_rx.at[2, 2, g])
        for p, (start, width, x_first) in enumerate(PIECES):
            columns = slice(start, start + width)
            left = sol[2, g].reshape(8 * HG, W)
            upd[g, :, :, columns] += product3(left, th[1, columns], tl[1, columns]).reshape(8, HG, width)
            lanes = pl.ds(start, width)
            if x_first:
                send(upd.at[g, pl.ds((1 - xl) * 4, 4), :, lanes], xa.at[g, p - 1], u_tx.at[0, g, p], u_rx.at[0, g, p], across)
            else:
                for d in (1, 2, 3):
                    for x in range(2):
                        send(upd.at[g, x * 4 + (z + d) % 4, :, lanes], zb.at[g, p // 3, d - 1, x],
                             u_tx.at[0, g, p], u_rx.at[0, g, p], z_dev(d))

    def middle(g):
        for p, (start, width, x_first) in enumerate(PIECES):
            columns = slice(start, start + width)
            lanes = pl.ds(start, width)
            if x_first:
                settle(xa.at[g, p - 1], u_rx.at[0, g, p])
                upd[g, pl.ds(xl * 4, 4), :, columns] += xa[g, p - 1]
                for d in (1, 2, 3):
                    send(upd.at[g, xl * 4 + (z + d) % 4, :, lanes], za.at[g, p - 1, d - 1],
                         u_tx.at[1, g, p], u_rx.at[1, g, p], z_dev(d))
            else:
                n = p // 3
                settle(zb.at[g, n], u_rx.at[0, g, p])
                for x in range(2):
                    terms = (zb[g, n, 0, x] + zb[g, n, 1, x]) + zb[g, n, 2, x]
                    upd[g, x * 4 + z, :, columns] += terms
                send(upd.at[g, (1 - xl) * 4 + z, :, lanes], xb.at[g, n], u_tx.at[1, g, p], u_rx.at[1, g, p], across)

    def finish(g):
        rows = slice(g * HG, (g + 1) * HG)
        for p, (start, width, x_first) in enumerate(PIECES):
            columns = slice(start, start + width)
            total = upd[g, q, :, columns]
            if x_first:
                settle(za.at[g, p - 1], u_rx.at[1, g, p])
                total = total + ((za[g, p - 1, 0] + za[g, p - 1, 1]) + za[g, p - 1, 2])
            else:
                settle(xb.at[g, p // 3], u_rx.at[1, g, p])
                total = total + xb[g, p // 3]
            updated_ref[rows, columns] = rhs[rows, columns] - total

    order = []
    for g in range(G):
        for s in range(3):
            begin = (4 * s + g) * STEP
            order += [(begin, multiply, (s, g)), (begin + 1.5 * STEP, sum_up, (s, g)), (begin + 2.6 * STEP, spread, (s, g))]
        begin = (12 + g) * STEP
        order += [(begin, second_trail, (g,)), (12 * STEP + 9 * (g + 1), middle, (g,)), (12 * STEP + 9 * (g + 1) + 10, finish, (g,))]
    order += [(0.1, ready_small, (1,)), (0.2, ready_small, (2,)), (1.1 * STEP, ready_trail, (0,)), (2.1 * STEP, ready_second, ()),
              (3.1 * STEP, ready_trail, (1,)), (11.9 * STEP, loads[5].wait, ())]
    order += [((7.1 + 0.5 * p) * STEP, first_trail, (p,)) for p in range(4)]
    for _, work, which in sorted(order, key=lambda entry: entry[0]):
        work(*which)

    for i in range(3):
        settle(sib_s.at[i], sib_tx.at[i])
    for i in range(2):
        settle(sib_t.at[i], sib_tx.at[3 + i])

    @pl.when(diagonal)
    def _():
        settle(xt.at[pl.ds(0, 15), pl.ds(0, 8)], x_tx.at[0])

    @pl.when(jnp.logical_not(diagonal))
    def _():
        settle(xt.at[:, pl.ds(0, 8)], x_tx.at[0])

    settle(x1b.at[pl.ds(0, 15)], x_tx.at[1])
    for g in range(G):
        settle(xt.at[:, pl.ds(0, 24), pl.ds(0, HL)], xg_tx.at[g])
        for s in range(3):
            settle(got.at[s, g], st_tx.at[0, s, g])

            @pl.when(diagonal)
            def _():
                settle(sol.at[s, g, pl.ds(0, 7), :, pl.ds(0, 128)], st_tx.at[1, s, g])

            @pl.when(jnp.logical_not(diagonal))
            def _():
                settle(sol.at[s, g, :, :, pl.ds(0, 128)], st_tx.at[1, s, g])

            settle(three_lanes(s, g), st_tx.at[2, s, g])
        for p, (_, _, x_first) in enumerate(PIECES):
            if x_first:
                settle(xa.at[g, p - 1], u_tx.at[0, g, p])
                settle(za.at[g, p - 1], u_tx.at[1, g, p])
            else:
                settle(zb.at[g, p // 3], u_tx.at[0, g, p])
                settle(xb.at[g, p // 3], u_tx.at[1, g, p])


def on_device(incident, diag_first, coupling, diag_second, trail_first, trail_second, trail_rhs):
    whole = pl.BlockSpec(memory_space=pltpu.VMEM)
    far = pl.BlockSpec(memory_space=pl.ANY)
    dma = pltpu.SemaphoreType.DMA
    return pl.pallas_call(
        kernel,
        out_shape=(jax.ShapeDtypeStruct((2, 64, W), F32), jax.ShapeDtypeStruct((64, TR), F32)),
        in_specs=[whole] + [far] * 6,
        out_specs=(whole, whole),
        scratch_shapes=[
            pltpu.VMEM((3, W, 256), F32),
            pltpu.VMEM((3, W, 256), F32),
            pltpu.VMEM((2, TR, 256), F32),
            pltpu.VMEM((2, TR, 256), F32),
            pltpu.VMEM((64, TR), F32),
            pltpu.VMEM((3, W, W), BF),
            pltpu.VMEM((3, W, W), BF),
            pltpu.VMEM((2, TR, W), BF),
            pltpu.VMEM((2, TR, W), BF),
            pltpu.VMEM((2, 32, 512), F32),
            pltpu.VMEM((16, 32, 512), F32),
            pltpu.VMEM((16, 32, 128), F32),
            pltpu.VMEM((2, 64, W), F32),
            pltpu.VMEM((3, G, 8, HG, W), F32),
            pltpu.VMEM((3, G, 7, HG, W), F32),
            pltpu.VMEM((3, G, HG, W), F32),
            pltpu.VMEM((3, G, 8, HG, W), F32),
            pltpu.VMEM((G, 8, HG, TR), F32),
            pltpu.VMEM((G, 2, 4, HG, XW), F32),
            pltpu.VMEM((G, 2, 3, HG, XW), F32),
            pltpu.VMEM((G, 2, 3, 2, HG, ZW), F32),
            pltpu.VMEM((G, 2, HG, ZW), F32),
            dma((6,)), dma((5,)), dma((5,)), dma((2,)), dma((2,)), dma((G,)), dma((G,)),
            dma((3, 3, G)), dma((3, 3, G)), dma((2, G, 4)), dma((2, G, 4)),
        ],
        compiler_params=pltpu.CompilerParams(
            collective_id=0, has_side_effects=True, vmem_limit_bytes=60 * 1024 * 1024
        ),
        name="solve",
    )(jnp.swapaxes(incident, 1, 2), diag_first, coupling, diag_second, trail_first, trail_second, trail_rhs)


def solution(mesh):
    split_all = P("rows", "cols")
    return jax.shard_map(
        on_device,
        mesh=mesh,
        in_specs=(P(None, None, ("rows", "cols")),) + (split_all,) * 5 + (P("cols", "rows"),),
        out_specs=(P(None, "cols", "rows"), P("cols", "rows")),
        check_vma=False,
    )
```

```python
import functools

import jax
import jax.numpy as jnp
from jax import lax
from jax.experimental import pallas as pl
from jax.experimental.pallas import tpu as pltpu
from jax.sharding import PartitionSpec as P

MESH = pl.DeviceIdType.MESH
BF = jnp.bfloat16
F32 = jnp.float32

G = 4
HG = 64 // G
W = 512
HL = 512 // G
TR = 2560
XW, ZW = 640, 640
PIECES = ((2 * XW, ZW, 0), (0, XW, 1), (XW, XW, 1), (2 * XW + ZW, ZW, 0))
STEP = 16
SKEW = 4
STAGES = 11, 16, 24


def split(x):
    hi = x.astype(BF)
    return hi, (x - hi.astype(F32)).astype(BF)


def product3(left, right_hi, right_lo):
    hi, lo = split(left)

    def dot(a, b):
        return lax.dot_general(a, b, (((1,), (1,)), ((), ())), preferred_element_type=F32)

    return dot(hi, right_hi) + (dot(hi, right_lo) + dot(lo, right_hi))


def kernel(
    incident_ref, d1_ref, c_ref, d2_ref, t1_ref, t2_ref, rhs_ref,
    solved_out, updated_out,
    x_ref, solved_ref, updated_ref,
    own_s, sib_s, own_t, sib_t, rhs,
    wh, wl, th, tl,
    xr, xt, x1b, x1s,
    part, got, summed, sol,
    upd, xa, xrel, za, zrel, zb, xb,
    loc, sib_tx, sib_rx, x_tx, x_rx, xg_tx, xg_rx, st_tx, st_rx, u_tx, u_rx, out_sem,
):
    r = lax.axis_index("rows")
    c = lax.axis_index("cols")
    y, xh = r // 2, r % 2
    q, k = c // 2, c % 2
    xl, z = q // 4, q % 4
    own_lanes = pl.ds(pl.multiple_of(k * 256, 256), 256)
    sib_lanes = pl.ds(pl.multiple_of((1 - k) * 256, 256), 256)
    sibling = (r, q * 2 + (1 - k))
    diagonal = r == q

    def send(src, dst, tx, rx, dev):
        pltpu.make_async_remote_copy(
            src_ref=src, dst_ref=dst, send_sem=tx, recv_sem=rx, device_id=dev, device_id_type=MESH
        ).start()

    def settle(ref, sem):
        pltpu.make_async_copy(ref, ref, sem).wait()

    first = pltpu.make_async_copy(incident_ref, x_ref, loc.at[6])
    first.start()
    own = [(d1_ref, own_s.at[0]), (c_ref, own_s.at[1]), (d2_ref, own_s.at[2]),
           (t1_ref, own_t.at[0]), (t2_ref, own_t.at[1]), (rhs_ref, rhs)]
    loads = [pltpu.make_async_copy(src, dst, loc.at[i]) for i, (src, dst) in enumerate(own)]
    for load in loads:
        load.start()

    barrier = pltpu.get_barrier_semaphore()
    plane = [(dq, dk) for dq in range(8) for dk in range(2) if (dq, dk) != (0, 0)]

    def plane_dev(dq, dk):
        return (r, ((q + dq) % 8) * 2 + (k + dk) % 2)

    def y_dev(d):
        return (((y + d) % 4) * 2 + xh, c)

    def greet(dev):
        pl.semaphore_signal(barrier, inc=1, device_id=dev, device_id_type=MESH)

    for dq, dk in plane:
        greet(plane_dev(dq, dk))
    for d in (1, 2, 3):
        greet(y_dev(d))
    for j in range(8):
        greet((q, j * 2 + (1 - k)))

        @pl.when(jnp.logical_not(jnp.logical_and(diagonal, j == q)))
        def _():
            greet((q, j * 2 + k))

    first.wait()
    per = 128 // HG
    place = lax.broadcasted_iota(jnp.int32, (32, 128), 1) // HG
    for core in range(2):
        for t in range(4):
            tile = None
            for j in range(per):
                chip = (t * per + j) % 8
                here = core * G + (t * per + j) // 8
                taken = x_ref[0, :, chip * 128 : chip * 128 + 128]
                shift = ((j - here) * HG) % 128
                if shift:
                    taken = pltpu.roll(taken, shift, 1)
                tile = taken if tile is None else jnp.where(place == j, taken, tile)
            xr[core, t] = tile.reshape(4, 8, 128)

    pl.semaphore_wait(barrier, 33 + jnp.where(diagonal, 0, 1))

    for dk in range(2):
        kk = (k + dk) % 2
        for jy in range(4):
            for jx in range(2):
                j = jy * 2 + jx
                src, dst = xr.at[kk, :, jy], xt.at[:, jy, c]
                if dk == 1:
                    send(src, dst, x_tx.at[0], x_rx.at[0], (j, r * 2 + kk))
                else:
                    me = jnp.logical_and(diagonal, r == j)

                    @pl.when(jnp.logical_not(me))
                    def _():
                        send(src, dst, x_tx.at[0], x_rx.at[0], (j, r * 2 + kk))

                    @pl.when(me)
                    def _():
                        pltpu.make_async_copy(src, dst, x_rx.at[0]).start()

    small = [d1_ref, c_ref, d2_ref]
    send(small[0], sib_s.at[0], sib_tx.at[0], sib_rx.at[0], sibling)

    def ready_small(i):
        loads[i].wait()
        wh[i, :, own_lanes], wl[i, :, own_lanes] = split(own_s[i])
        settle(sib_s.at[i], sib_rx.at[i])
        wh[i, :, sib_lanes], wl[i, :, sib_lanes] = split(sib_s[i])

    def ready_trail(i):
        loads[3 + i].wait()
        settle(sib_t.at[i], sib_rx.at[3 + i])

        @pl.loop(0, 20)
        def _(n):
            rows = pl.ds(pl.multiple_of(n * 128, 128), 128)
            th[i, rows, own_lanes], tl[i, rows, own_lanes] = split(own_t[i, rows, :])
            th[i, rows, sib_lanes], tl[i, rows, sib_lanes] = split(sib_t[i, rows, :])

    ready_small(0)
    settle(xt.at[:, y], x_rx.at[0])
    for g in range(G):
        for d in (1, 2, 3):
            block = xt.at[g, y]
            send(block, block, xg_tx.at[g], xg_rx.at[g], y_dev(d))
    send(small[1], sib_s.at[1], sib_tx.at[1], sib_rx.at[1], sibling)
    for dq, dk in plane:
        lanes = pl.ds(pl.multiple_of(((q + dq) % 8) * 128, 128), 128)
        send(x_ref.at[1, :, lanes], x1b.at[c], x_tx.at[1], x_rx.at[1], plane_dev(dq, dk))
    x1b[c] = x_ref[1, :, pl.ds(pl.multiple_of(q * 128, 128), 128)]
    send(small[2], sib_s.at[2], sib_tx.at[2], sib_rx.at[2], sibling)
    for i, t_ref in enumerate((t1_ref, t2_ref)):
        send(t_ref, sib_t.at[i], sib_tx.at[3 + i], sib_rx.at[3 + i], sibling)

    def three_pieces(s, g):
        return sol.at[s, g, pl.ds(0, 3)]

    def solved_of(s, g):
        return jnp.concatenate([sol[s, g, piece].reshape(8 * HG, 128) for piece in range(4)], axis=1)

    def multiply(s, g):
        if s == 0:
            settle(xt.at[g, pl.ds(0, 3)], xg_rx.at[g])
            left = jnp.concatenate([xt[g, :, held].reshape(32, HL) for held in range(16)], axis=0).T
        else:
            settle(three_pieces(s - 1, g), st_rx.at[2, s - 1, g])
            left = solved_of(s - 1, g)
        out = product3(left, wh[s], wl[s])
        part[s, g] = out.reshape(8, HG, W)
        for d in range(1, 8):
            to = (q + d) % 8
            send(part.at[s, g, to], got.at[s, g, d - 1], st_tx.at[0, s, g], st_rx.at[0, s, g], (r, to * 2 + k))

    def sum_up(s, g):
        settle(got.at[s, g], st_rx.at[0, s, g])
        total = part[s, g, q]
        for d in range(7):
            total = total + got[s, g, d]
        rows = pl.ds(g * HG, HG)
        if s == 1:
            total = x1s[k, rows] - total
        else:
            solved_ref[s // 2, rows] = total
            pltpu.make_async_copy(solved_ref.at[s // 2, rows], solved_out.at[s // 2, rows], out_sem.at[s // 2, g]).start()
        for piece in range(4):
            summed[s, g, piece] = total[:, piece * 128 : piece * 128 + 128]
        for jy in range(4):
            for jx in range(2):
                j = jy * 2 + jx
                src, dst = summed.at[s, g, jy], sol.at[s, g, jy, q]
                me = jnp.logical_and(diagonal, r == j)

                @pl.when(jnp.logical_not(me))
                def _():
                    send(src, dst, st_tx.at[1, s, g], st_rx.at[1, s, g], (j, r * 2 + k))

                @pl.when(me)
                def _():
                    pltpu.make_async_copy(src, dst, st_rx.at[1, s, g]).start()

    def spread(s, g):
        block = sol.at[s, g, y]
        settle(block, st_rx.at[1, s, g])
        for d in (1, 2, 3):
            send(block, block, st_tx.at[2, s, g], st_rx.at[2, s, g], y_dev(d))

    def ready_second():
        settle(x1b.at[pl.ds(0, 15)], x_rx.at[1])
        x1s[...] = x1b[...].reshape(512, 128).T.reshape(2, 64, W)

    def first_trail(pair, p):
        start, width, _ = PIECES[p]
        columns = slice(start, start + width)
        both = slice(2 * pair, 2 * pair + 2)
        left = jnp.concatenate([solved_of(0, 2 * pair), solved_of(0, 2 * pair + 1)], axis=0)
        upd[both, :, :, columns] = product3(left, th[0, columns], tl[0, columns]).reshape(2, 8, HG, width)

    across = (r, ((1 - xl) * 4 + z) * 2 + k)

    def z_dev(d):
        return (r, (xl * 4 + (z + d) % 4) * 2 + k)

    ways = (1, 3)
    sides = ((z + 1) % 4, (z + 3) % 4)
    opposite = (z + 2) % 4

    def second_trail(g):
        settle(three_pieces(2, g), st_rx.at[2, 2, g])
        left = solved_of(2, g)
        for p, (start, width, x_first) in enumerate(PIECES):
            columns = slice(start, start + width)
            upd[g, :, :, columns] += product3(left, th[1, columns], tl[1, columns]).reshape(8, HG, width)
            lanes = pl.ds(start, width)
            if x_first:
                send(upd.at[g, pl.ds((1 - xl) * 4, 4), :, lanes], xa.at[g, p - 1], u_tx.at[0, g, p], u_rx.at[0, g, p], across)
            else:
                n = p // 3
                for x in range(2):
                    send(upd.at[g, x * 4 + opposite, :, lanes], zrel.at[g, n, x], u_tx.at[0, g, p], u_rx.at[0, g, p], z_dev(ways[x]))
                for x in range(2):
                    send(upd.at[g, (1 - x) * 4 + sides[x], :, lanes], zb.at[g, n, x, 1 - x],
                         u_tx.at[1, g, p], u_rx.at[1, g, p], z_dev(ways[x]))

    def middle(g):
        for p, (start, width, x_first) in enumerate(PIECES):
            columns = slice(start, start + width)
            lanes = pl.ds(start, width)
            if x_first:
                settle(xa.at[g, p - 1], u_rx.at[0, g, p])
                upd[g, pl.ds(xl * 4, 4), :, columns] += xa[g, p - 1]
                for h in range(2):
                    rows = pl.ds(h * (HG // 2), HG // 2)
                    send(upd.at[g, xl * 4 + opposite, rows, lanes], xrel.at[g, p - 1, h],
                         u_tx.at[1, g, p], u_rx.at[1, g, p], z_dev(ways[h]))
                for h in range(2):
                    rows = pl.ds((1 - h) * (HG // 2), HG // 2)
                    send(upd.at[g, xl * 4 + sides[h], rows, lanes], za.at[g, p - 1, h, rows],
                         u_tx.at[2, g, p], u_rx.at[2, g, p], z_dev(ways[h]))
            else:
                n = p // 3
                settle(zrel.at[g, n], u_rx.at[0, g, p])
                for x in range(2):
                    upd[g, x * 4 + sides[x], :, columns] += zrel[g, n, x]
                    send(upd.at[g, x * 4 + sides[x], :, lanes], zb.at[g, n, x, x], u_tx.at[1, g, p], u_rx.at[1, g, p], z_dev(ways[x]))

    def later(g):
        for p, (start, width, x_first) in enumerate(PIECES):
            columns = slice(start, start + width)
            lanes = pl.ds(start, width)
            if x_first:
                settle(xrel.at[g, p - 1], u_rx.at[1, g, p])
                for h in range(2):
                    half = slice(h * (HG // 2), (h + 1) * (HG // 2))
                    rows = pl.ds(h * (HG // 2), HG // 2)
                    upd[g, xl * 4 + sides[h], half, columns] += xrel[g, p - 1, h]
                    send(upd.at[g, xl * 4 + sides[h], rows, lanes], za.at[g, p - 1, h, rows],
                         u_tx.at[2, g, p], u_rx.at[2, g, p], z_dev(ways[h]))
            else:
                n = p // 3
                settle(zb.at[g, n], u_rx.at[1, g, p])
                for x in range(2):
                    upd[g, x * 4 + z, :, columns] += zb[g, n, 0, x] + zb[g, n, 1, x]
                send(upd.at[g, (1 - xl) * 4 + z, :, lanes], xb.at[g, n], u_tx.at[2, g, p], u_rx.at[2, g, p], across)

    def finish(g):
        rows = pl.ds(g * HG, HG)
        for p, (start, width, x_first) in enumerate(PIECES):
            columns = slice(start, start + width)
            total = upd[g, q, :, columns]
            if x_first:
                settle(za.at[g, p - 1], u_rx.at[2, g, p])
                total = total + (za[g, p - 1, 0] + za[g, p - 1, 1])
            else:
                settle(xb.at[g, p // 3], u_rx.at[2, g, p])
                total = total + xb[g, p // 3]
            updated_ref[rows, columns] = rhs[rows, columns] - total
        pltpu.make_async_copy(updated_ref.at[rows], updated_out.at[rows], out_sem.at[2, g]).start()

    order = []
    for g in range(G):
        for s in range(3):
            begin = s * STEP + g * SKEW
            order += [(begin, multiply, (s, g)), (begin + 6, sum_up, (s, g)), (begin + 10.4, spread, (s, g))]
        begin = 3 * STEP + g * SKEW
        order += [(begin, second_trail, (g,)), (begin + STAGES[0], middle, (g,)),
                  (begin + STAGES[1], later, (g,)), (begin + STAGES[2], finish, (g,))]
    order += [(0.1, ready_small, (1,)), (0.2, ready_small, (2,)), (4.4, ready_trail, (0,)), (8.4, ready_second, ()),
              (12.4, ready_trail, (1,)), (3 * STEP - 0.4, loads[5].wait, ())]
    for pair in range(2):
        order += [(STEP + (2 * pair + 1) * SKEW + 0.4 + 2 * p, first_trail, (pair, p)) for p in range(4)]
    for _, work, which in sorted(order, key=lambda entry: entry[0]):
        work(*which)

    for i in range(3):
        settle(sib_s.at[i], sib_tx.at[i])
    for i in range(2):
        settle(sib_t.at[i], sib_tx.at[3 + i])

    @pl.when(diagonal)
    def _():
        settle(xt.at[:, 0, pl.ds(0, 15)], x_tx.at[0])

    @pl.when(jnp.logical_not(diagonal))
    def _():
        settle(xt.at[:, 0], x_tx.at[0])

    settle(x1b.at[pl.ds(0, 15)], x_tx.at[1])
    for g in range(G):
        rows = pl.ds(g * HG, HG)
        settle(solved_ref.at[0, rows], out_sem.at[0, g])
        settle(solved_ref.at[1, rows], out_sem.at[1, g])
        settle(updated_ref.at[rows], out_sem.at[2, g])
        settle(xt.at[g, pl.ds(0, 3)], xg_tx.at[g])
        for s in range(3):
            settle(got.at[s, g], st_tx.at[0, s, g])

            @pl.when(diagonal)
            def _():
                settle(sol.at[s, g, 0, pl.ds(0, 7)], st_tx.at[1, s, g])

            @pl.when(jnp.logical_not(diagonal))
            def _():
                settle(sol.at[s, g, 0], st_tx.at[1, s, g])

            settle(three_pieces(s, g), st_tx.at[2, s, g])
        for p, (_, _, x_first) in enumerate(PIECES):
            if x_first:
                settle(xa.at[g, p - 1], u_tx.at[0, g, p])
                settle(xrel.at[g, p - 1], u_tx.at[1, g, p])
                settle(za.at[g, p - 1], u_tx.at[2, g, p])
            else:
                settle(zrel.at[g, p // 3], u_tx.at[0, g, p])
                settle(zb.at[g, p // 3], u_tx.at[1, g, p])
                settle(xb.at[g, p // 3], u_tx.at[2, g, p])


def hand_over(solved_in, updated_in, solved_out, updated_out, sems):
    copies = [
        pltpu.make_async_copy(solved_in, solved_out, sems.at[0]),
        pltpu.make_async_copy(updated_in, updated_out, sems.at[1]),
    ]
    for copy in copies:
        copy.start()
    for copy in copies:
        copy.wait()


def on_device(incident, diag_first, coupling, diag_second, trail_first, trail_second, trail_rhs):
    far = pl.BlockSpec(memory_space=pl.ANY)
    dma = pltpu.SemaphoreType.DMA
    shapes = (jax.ShapeDtypeStruct((2, 64, W), F32), jax.ShapeDtypeStruct((64, TR), F32))
    results = pl.pallas_call(
        kernel,
        out_shape=shapes,
        in_specs=[far] * 7,
        out_specs=(far, far),
        scratch_shapes=[
            pltpu.VMEM((2, 32, 1024), F32),
            pltpu.VMEM((2, 64, W), F32),
            pltpu.VMEM((64, TR), F32),
            pltpu.VMEM((3, W, 256), F32),
            pltpu.VMEM((3, W, 256), F32),
            pltpu.VMEM((2, TR, 256), F32),
            pltpu.VMEM((2, TR, 256), F32),
            pltpu.VMEM((64, TR), F32),
            pltpu.VMEM((3, W, W), BF),
            pltpu.VMEM((3, W, W), BF),
            pltpu.VMEM((2, TR, W), BF),
            pltpu.VMEM((2, TR, W), BF),
            pltpu.VMEM((2, G, 4, 8, HL), F32),
            pltpu.VMEM((G, 4, 16, 8, HL), F32),
            pltpu.VMEM((16, 32, 128), F32),
            pltpu.VMEM((2, 64, W), F32),
            pltpu.VMEM((3, G, 8, HG, W), F32),
            pltpu.VMEM((3, G, 7, HG, W), F32),
            pltpu.VMEM((3, G, 4, HG, 128), F32),
            pltpu.VMEM((3, G, 4, 8, HG, 128), F32),
            pltpu.VMEM((G, 8, HG, TR), F32),
            pltpu.VMEM((G, 2, 4, HG, XW), F32),
            pltpu.VMEM((G, 2, 2, HG // 2, XW), F32),
            pltpu.VMEM((G, 2, 2, HG, XW), F32),
            pltpu.VMEM((G, 2, 2, HG, ZW), F32),
            pltpu.VMEM((G, 2, 2, 2, HG, ZW), F32),
            pltpu.VMEM((G, 2, HG, ZW), F32),
            dma((7,)), dma((5,)), dma((5,)), dma((2,)), dma((2,)), dma((G,)), dma((G,)),
            dma((3, 3, G)), dma((3, 3, G)), dma((3, G, 4)), dma((3, G, 4)), dma((3, G)),
        ],
        compiler_params=pltpu.CompilerParams(
            collective_id=0, has_side_effects=True, vmem_limit_bytes=60 * 1024 * 1024
        ),
        name="solve",
    )(jnp.swapaxes(incident, 1, 2), diag_first, coupling, diag_second, trail_first, trail_second, trail_rhs)
    return pl.pallas_call(
        hand_over,
        out_shape=shapes,
        in_specs=[pl.BlockSpec(memory_space=pltpu.VMEM)] * 2,
        out_specs=(far, far),
        scratch_shapes=[dma((2,))],
        name="hand_over",
    )(*results)


def solution(mesh):
    split_all = P("rows", "cols")
    return jax.shard_map(
        on_device,
        mesh=mesh,
        in_specs=(P(None, None, ("rows", "cols")),) + (split_all,) * 5 + (P("cols", "rows"),),
        out_specs=(P(None, "cols", "rows"), P("cols", "rows")),
        check_vma=False,
    )
```

```python
import functools

import jax
import jax.numpy as jnp
from jax import lax
from jax.experimental import pallas as pl
from jax.experimental.pallas import tpu as pltpu
from jax.sharding import PartitionSpec as P

MESH = pl.DeviceIdType.MESH
BF = jnp.bfloat16
F32 = jnp.float32

G = 4
HG = 64 // G
W = 512
HL = 512 // G
TR = 2560
XW, ZW = 640, 640
PIECES = ((2 * XW, ZW, 0), (0, XW, 1), (XW, XW, 1), (2 * XW + ZW, ZW, 0))
STEP = 20
SKEW = 4
STAGES = 11, 17.5, 26.5


def split(x):
    hi = x.astype(BF)
    return hi, (x - hi.astype(F32)).astype(BF)


def product3(left, right_hi, right_lo):
    hi, lo = split(left)

    def dot(a, b):
        return lax.dot_general(a, b, (((1,), (1,)), ((), ())), preferred_element_type=F32)

    return dot(hi, right_hi) + (dot(hi, right_lo) + dot(lo, right_hi))


def kernel(
    incident_ref, d1_ref, c_ref, d2_ref, t1_ref, t2_ref, rhs_ref,
    solved_out, updated_out,
    x_ref, solved_ref, updated_ref,
    own_s, sib_s, own_t, sib_t, rhs,
    wh, wl, th, tl,
    xr, xt, x1b, x1s,
    part, got, summed, sol,
    upd, xa, xrel, za, zrel, zb, xb,
    loc, sib_tx, sib_rx, x_tx, x_rx, xg_tx, xg_rx, st_tx, st_rx, u_tx, u_rx, out_sem,
):
    r = lax.axis_index("rows")
    c = lax.axis_index("cols")
    y, xh = r // 2, r % 2
    q, k = c // 2, c % 2
    xl, z = q // 4, q % 4
    own_lanes = pl.ds(pl.multiple_of(k * 256, 256), 256)
    sib_lanes = pl.ds(pl.multiple_of((1 - k) * 256, 256), 256)
    sibling = (r, q * 2 + (1 - k))
    diagonal = r == q

    def send(src, dst, tx, rx, dev):
        pltpu.make_async_remote_copy(
            src_ref=src, dst_ref=dst, send_sem=tx, recv_sem=rx, device_id=dev, device_id_type=MESH
        ).start()

    def settle(ref, sem):
        pltpu.make_async_copy(ref, ref, sem).wait()

    first = pltpu.make_async_copy(incident_ref, x_ref, loc.at[6])
    first.start()
    own = [(d1_ref, own_s.at[0]), (c_ref, own_s.at[1]), (d2_ref, own_s.at[2]),
           (t1_ref, own_t.at[0]), (t2_ref, own_t.at[1]), (rhs_ref, rhs)]
    loads = [pltpu.make_async_copy(src, dst, loc.at[i]) for i, (src, dst) in enumerate(own)]
    for load in loads:
        load.start()

    barrier = pltpu.get_barrier_semaphore()
    plane = [(dq, dk) for dq in range(8) for dk in range(2) if (dq, dk) != (0, 0)]

    def plane_dev(dq, dk):
        return (r, ((q + dq) % 8) * 2 + (k + dk) % 2)

    def y_dev(d):
        return (((y + d) % 4) * 2 + xh, c)

    def greet(dev):
        pl.semaphore_signal(barrier, inc=1, device_id=dev, device_id_type=MESH)

    for dq, dk in plane:
        greet(plane_dev(dq, dk))
    for d in (1, 2, 3):
        greet(y_dev(d))
    for j in range(8):
        greet((q, j * 2 + (1 - k)))

        @pl.when(jnp.logical_not(jnp.logical_and(diagonal, j == q)))
        def _():
            greet((q, j * 2 + k))

    first.wait()
    per = 128 // HG
    place = lax.broadcasted_iota(jnp.int32, (32, 128), 1) // HG
    for core in range(2):
        for t in range(4):
            tile = None
            for j in range(per):
                chip = (t * per + j) % 8
                here = core * G + (t * per + j) // 8
                taken = x_ref[0, :, chip * 128 : chip * 128 + 128]
                shift = ((j - here) * HG) % 128
                if shift:
                    taken = pltpu.roll(taken, shift, 1)
                tile = taken if tile is None else jnp.where(place == j, taken, tile)
            xr[core, t] = tile.reshape(4, 8, 128)

    pl.semaphore_wait(barrier, 33 + jnp.where(diagonal, 0, 1))

    for dk in range(2):
        kk = (k + dk) % 2
        for jy in range(4):
            for jx in range(2):
                j = jy * 2 + jx
                src, dst = xr.at[kk, :, jy], xt.at[:, jy, c]
                if dk == 1:
                    send(src, dst, x_tx.at[0], x_rx.at[0], (j, r * 2 + kk))
                else:
                    me = jnp.logical_and(diagonal, r == j)

                    @pl.when(jnp.logical_not(me))
                    def _():
                        send(src, dst, x_tx.at[0], x_rx.at[0], (j, r * 2 + kk))

                    @pl.when(me)
                    def _():
                        pltpu.make_async_copy(src, dst, x_rx.at[0]).start()

    small = [d1_ref, c_ref, d2_ref]
    send(small[0], sib_s.at[0], sib_tx.at[0], sib_rx.at[0], sibling)

    def ready_small(i):
        loads[i].wait()
        wh[i, :, own_lanes], wl[i, :, own_lanes] = split(own_s[i])
        settle(sib_s.at[i], sib_rx.at[i])
        wh[i, :, sib_lanes], wl[i, :, sib_lanes] = split(sib_s[i])

    def ready_trail(i):
        loads[3 + i].wait()
        settle(sib_t.at[i], sib_rx.at[3 + i])

        @pl.loop(0, 20)
        def _(n):
            rows = pl.ds(pl.multiple_of(n * 128, 128), 128)
            th[i, rows, own_lanes], tl[i, rows, own_lanes] = split(own_t[i, rows, :])
            th[i, rows, sib_lanes], tl[i, rows, sib_lanes] = split(sib_t[i, rows, :])

    ready_small(0)
    settle(xt.at[:, y], x_rx.at[0])
    for g in range(G):
        for d in (1, 2, 3):
            block = xt.at[g, y]
            send(block, block, xg_tx.at[g], xg_rx.at[g], y_dev(d))
    send(small[1], sib_s.at[1], sib_tx.at[1], sib_rx.at[1], sibling)
    for dq, dk in plane:
        lanes = pl.ds(pl.multiple_of(((q + dq) % 8) * 128, 128), 128)
        send(x_ref.at[1, :, lanes], x1b.at[c], x_tx.at[1], x_rx.at[1], plane_dev(dq, dk))
    x1b[c] = x_ref[1, :, pl.ds(pl.multiple_of(q * 128, 128), 128)]
    send(small[2], sib_s.at[2], sib_tx.at[2], sib_rx.at[2], sibling)
    for i, t_ref in enumerate((t1_ref, t2_ref)):
        send(t_ref, sib_t.at[i], sib_tx.at[3 + i], sib_rx.at[3 + i], sibling)

    def three_pieces(s, g):
        return sol.at[s, g, pl.ds(0, 3)]

    def solved_of(s, g):
        return jnp.concatenate([sol[s, g, piece].reshape(8 * HG, 128) for piece in range(4)], axis=1)

    def multiply(s, g):
        if s == 0:
            settle(xt.at[g, pl.ds(0, 3)], xg_rx.at[g])
            left = jnp.concatenate([xt[g, :, held].reshape(32, HL) for held in range(16)], axis=0).T
        else:
            settle(three_pieces(s - 1, g), st_rx.at[2, s - 1, g])
            left = solved_of(s - 1, g)
        out = product3(left, wh[s], wl[s])
        part[s, g] = out.reshape(8, HG, W)
        for d in range(1, 8):
            to = (q + d) % 8
            send(part.at[s, g, to], got.at[s, g, d - 1], st_tx.at[0, s, g], st_rx.at[0, s, g], (r, to * 2 + k))

    def sum_up(s, g):
        settle(got.at[s, g], st_rx.at[0, s, g])
        total = part[s, g, q]
        for d in range(7):
            total = total + got[s, g, d]
        rows = pl.ds(g * HG, HG)
        if s == 1:
            total = x1s[k, rows] - total
        else:
            solved_ref[s // 2, rows] = total
            pltpu.make_async_copy(solved_ref.at[s // 2, rows], solved_out.at[s // 2, rows], out_sem.at[s // 2, g]).start()
        for piece in range(4):
            summed[s, g, piece] = total[:, piece * 128 : piece * 128 + 128]
        for jy in range(4):
            for jx in range(2):
                j = jy * 2 + jx
                src, dst = summed.at[s, g, jy], sol.at[s, g, jy, q]
                me = jnp.logical_and(diagonal, r == j)

                @pl.when(jnp.logical_not(me))
                def _():
                    send(src, dst, st_tx.at[1, s, g], st_rx.at[1, s, g], (j, r * 2 + k))

                @pl.when(me)
                def _():
                    pltpu.make_async_copy(src, dst, st_rx.at[1, s, g]).start()

    def spread(s, g):
        block = sol.at[s, g, y]
        settle(block, st_rx.at[1, s, g])
        for d in (1, 2, 3):
            send(block, block, st_tx.at[2, s, g], st_rx.at[2, s, g], y_dev(d))

    def ready_second():
        settle(x1b.at[pl.ds(0, 15)], x_rx.at[1])
        x1s[...] = x1b[...].reshape(512, 128).T.reshape(2, 64, W)

    def first_trail(pair, p):
        start, width, _ = PIECES[p]
        columns = slice(start, start + width)
        both = slice(2 * pair, 2 * pair + 2)
        left = jnp.concatenate([solved_of(0, 2 * pair), solved_of(0, 2 * pair + 1)], axis=0)
        upd[both, :, :, columns] = product3(left, th[0, columns], tl[0, columns]).reshape(2, 8, HG, width)

    across = (r, ((1 - xl) * 4 + z) * 2 + k)

    def z_dev(d):
        return (r, (xl * 4 + (z + d) % 4) * 2 + k)

    ways = (1, 3)
    sides = ((z + 1) % 4, (z + 3) % 4)
    opposite = (z + 2) % 4

    def second_trail(g):
        settle(three_pieces(2, g), st_rx.at[2, 2, g])
        left = solved_of(2, g)
        for p, (start, width, x_first) in enumerate(PIECES):
            columns = slice(start, start + width)
            upd[g, :, :, columns] += product3(left, th[1, columns], tl[1, columns]).reshape(8, HG, width)
            lanes = pl.ds(start, width)
            if x_first:
                send(upd.at[g, pl.ds((1 - xl) * 4, 4), :, lanes], xa.at[g, p - 1], u_tx.at[0, g, p], u_rx.at[0, g, p], across)
            else:
                n = p // 3
                for x in range(2):
                    send(upd.at[g, x * 4 + opposite, :, lanes], zrel.at[g, n, x], u_tx.at[0, g, p], u_rx.at[0, g, p], z_dev(ways[x]))
                for x in range(2):
                    send(upd.at[g, (1 - x) * 4 + sides[x], :, lanes], zb.at[g, n, x, 1 - x],
                         u_tx.at[1, g, p], u_rx.at[1, g, p], z_dev(ways[x]))

    def middle(g):
        for p, (start, width, x_first) in enumerate(PIECES):
            columns = slice(start, start + width)
            lanes = pl.ds(start, width)
            if x_first:
                settle(xa.at[g, p - 1], u_rx.at[0, g, p])
                upd[g, pl.ds(xl * 4, 4), :, columns] += xa[g, p - 1]
                for h in range(2):
                    rows = pl.ds(h * (HG // 2), HG // 2)
                    send(upd.at[g, xl * 4 + opposite, rows, lanes], xrel.at[g, p - 1, h],
                         u_tx.at[1, g, p], u_rx.at[1, g, p], z_dev(ways[h]))
                for h in range(2):
                    rows = pl.ds((1 - h) * (HG // 2), HG // 2)
                    send(upd.at[g, xl * 4 + sides[h], rows, lanes], za.at[g, p - 1, h, rows],
                         u_tx.at[2, g, p], u_rx.at[2, g, p], z_dev(ways[h]))
            else:
                n = p // 3
                settle(zrel.at[g, n], u_rx.at[0, g, p])
                for x in range(2):
                    upd[g, x * 4 + sides[x], :, columns] += zrel[g, n, x]
                    send(upd.at[g, x * 4 + sides[x], :, lanes], zb.at[g, n, x, x], u_tx.at[1, g, p], u_rx.at[1, g, p], z_dev(ways[x]))

    def later(g):
        for p, (start, width, x_first) in enumerate(PIECES):
            columns = slice(start, start + width)
            lanes = pl.ds(start, width)
            if x_first:
                settle(xrel.at[g, p - 1], u_rx.at[1, g, p])
                for h in range(2):
                    half = slice(h * (HG // 2), (h + 1) * (HG // 2))
                    rows = pl.ds(h * (HG // 2), HG // 2)
                    upd[g, xl * 4 + sides[h], half, columns] += xrel[g, p - 1, h]
                    send(upd.at[g, xl * 4 + sides[h], rows, lanes], za.at[g, p - 1, h, rows],
                         u_tx.at[2, g, p], u_rx.at[2, g, p], z_dev(ways[h]))
            else:
                n = p // 3
                settle(zb.at[g, n], u_rx.at[1, g, p])
                for x in range(2):
                    upd[g, x * 4 + z, :, columns] += zb[g, n, 0, x] + zb[g, n, 1, x]
                send(upd.at[g, (1 - xl) * 4 + z, :, lanes], xb.at[g, n], u_tx.at[2, g, p], u_rx.at[2, g, p], across)

    def finish(g):
        rows = pl.ds(g * HG, HG)
        for p, (start, width, x_first) in enumerate(PIECES):
            columns = slice(start, start + width)
            total = upd[g, q, :, columns]
            if x_first:
                settle(za.at[g, p - 1], u_rx.at[2, g, p])
                total = total + (za[g, p - 1, 0] + za[g, p - 1, 1])
            else:
                settle(xb.at[g, p // 3], u_rx.at[2, g, p])
                total = total + xb[g, p // 3]
            updated_ref[rows, columns] = rhs[rows, columns] - total
        pltpu.make_async_copy(updated_ref.at[rows], updated_out.at[rows], out_sem.at[2, g]).start()

    order = []
    for g in range(G):
        for s in range(3):
            begin = s * STEP + g * SKEW
            order += [(begin, multiply, (s, g)), (begin + 6.4, sum_up, (s, g)), (begin + 12.4, spread, (s, g))]
        begin = 3 * STEP + g * SKEW
        order += [(begin, second_trail, (g,)), (begin + STAGES[0], middle, (g,)),
                  (begin + STAGES[1], later, (g,)), (begin + STAGES[2], finish, (g,))]
    order += [(0.1, ready_small, (1,)), (0.2, ready_small, (2,)), (4.4, ready_trail, (0,)), (8.4, ready_second, ()),
              (12.4, ready_trail, (1,)), (3 * STEP - 0.4, loads[5].wait, ())]
    for pair in range(2):
        order += [(STEP + (2 * pair + 1) * SKEW + 0.4 + 2 * p, first_trail, (pair, p)) for p in range(4)]
    for _, work, which in sorted(order, key=lambda entry: entry[0]):
        work(*which)

    for i in range(3):
        settle(sib_s.at[i], sib_tx.at[i])
    for i in range(2):
        settle(sib_t.at[i], sib_tx.at[3 + i])

    @pl.when(diagonal)
    def _():
        settle(xt.at[:, 0, pl.ds(0, 15)], x_tx.at[0])

    @pl.when(jnp.logical_not(diagonal))
    def _():
        settle(xt.at[:, 0], x_tx.at[0])

    settle(x1b.at[pl.ds(0, 15)], x_tx.at[1])
    for g in range(G):
        rows = pl.ds(g * HG, HG)
        settle(solved_ref.at[0, rows], out_sem.at[0, g])
        settle(solved_ref.at[1, rows], out_sem.at[1, g])
        settle(updated_ref.at[rows], out_sem.at[2, g])
        settle(xt.at[g, pl.ds(0, 3)], xg_tx.at[g])
        for s in range(3):
            settle(got.at[s, g], st_tx.at[0, s, g])

            @pl.when(diagonal)
            def _():
                settle(sol.at[s, g, 0, pl.ds(0, 7)], st_tx.at[1, s, g])

            @pl.when(jnp.logical_not(diagonal))
            def _():
                settle(sol.at[s, g, 0], st_tx.at[1, s, g])

            settle(three_pieces(s, g), st_tx.at[2, s, g])
        for p, (_, _, x_first) in enumerate(PIECES):
            if x_first:
                settle(xa.at[g, p - 1], u_tx.at[0, g, p])
                settle(xrel.at[g, p - 1], u_tx.at[1, g, p])
                settle(za.at[g, p - 1], u_tx.at[2, g, p])
            else:
                settle(zrel.at[g, p // 3], u_tx.at[0, g, p])
                settle(zb.at[g, p // 3], u_tx.at[1, g, p])
                settle(xb.at[g, p // 3], u_tx.at[2, g, p])


def hand_over(solved_in, updated_in, solved_out, updated_out, sems):
    copies = [
        pltpu.make_async_copy(solved_in, solved_out, sems.at[0]),
        pltpu.make_async_copy(updated_in, updated_out, sems.at[1]),
    ]
    for copy in copies:
        copy.start()
    for copy in copies:
        copy.wait()


def on_device(incident, diag_first, coupling, diag_second, trail_first, trail_second, trail_rhs):
    far = pl.BlockSpec(memory_space=pl.ANY)
    dma = pltpu.SemaphoreType.DMA
    shapes = (jax.ShapeDtypeStruct((2, 64, W), F32), jax.ShapeDtypeStruct((64, TR), F32))
    results = pl.pallas_call(
        kernel,
        out_shape=shapes,
        in_specs=[far] * 7,
        out_specs=(far, far),
        scratch_shapes=[
            pltpu.VMEM((2, 32, 1024), F32),
            pltpu.VMEM((2, 64, W), F32),
            pltpu.VMEM((64, TR), F32),
            pltpu.VMEM((3, W, 256), F32),
            pltpu.VMEM((3, W, 256), F32),
            pltpu.VMEM((2, TR, 256), F32),
            pltpu.VMEM((2, TR, 256), F32),
            pltpu.VMEM((64, TR), F32),
            pltpu.VMEM((3, W, W), BF),
            pltpu.VMEM((3, W, W), BF),
            pltpu.VMEM((2, TR, W), BF),
            pltpu.VMEM((2, TR, W), BF),
            pltpu.VMEM((2, G, 4, 8, HL), F32),
            pltpu.VMEM((G, 4, 16, 8, HL), F32),
            pltpu.VMEM((16, 32, 128), F32),
            pltpu.VMEM((2, 64, W), F32),
            pltpu.VMEM((3, G, 8, HG, W), F32),
            pltpu.VMEM((3, G, 7, HG, W), F32),
            pltpu.VMEM((3, G, 4, HG, 128), F32),
            pltpu.VMEM((3, G, 4, 8, HG, 128), F32),
            pltpu.VMEM((G, 8, HG, TR), F32),
            pltpu.VMEM((G, 2, 4, HG, XW), F32),
            pltpu.VMEM((G, 2, 2, HG // 2, XW), F32),
            pltpu.VMEM((G, 2, 2, HG, XW), F32),
            pltpu.VMEM((G, 2, 2, HG, ZW), F32),
            pltpu.VMEM((G, 2, 2, 2, HG, ZW), F32),
            pltpu.VMEM((G, 2, HG, ZW), F32),
            dma((7,)), dma((5,)), dma((5,)), dma((2,)), dma((2,)), dma((G,)), dma((G,)),
            dma((3, 3, G)), dma((3, 3, G)), dma((3, G, 4)), dma((3, G, 4)), dma((3, G)),
        ],
        compiler_params=pltpu.CompilerParams(
            collective_id=0, has_side_effects=True, vmem_limit_bytes=60 * 1024 * 1024
        ),
        name="solve",
    )(jnp.swapaxes(incident, 1, 2), diag_first, coupling, diag_second, trail_first, trail_second, trail_rhs)
    return pl.pallas_call(
        hand_over,
        out_shape=shapes,
        in_specs=[pl.BlockSpec(memory_space=pltpu.VMEM)] * 2,
        out_specs=(far, far),
        scratch_shapes=[dma((2,))],
        name="hand_over",
    )(*results)


def solution(mesh):
    split_all = P("rows", "cols")
    return jax.shard_map(
        on_device,
        mesh=mesh,
        in_specs=(P(None, None, ("rows", "cols")),) + (split_all,) * 5 + (P("cols", "rows"),),
        out_specs=(P(None, "cols", "rows"), P("cols", "rows")),
        check_vma=False,
    )
```

```python
import functools

import jax
import jax.numpy as jnp
from jax import lax
from jax.experimental import pallas as pl
from jax.experimental.pallas import tpu as pltpu
from jax.sharding import PartitionSpec as P

MESH = pl.DeviceIdType.MESH
BF = jnp.bfloat16
F32 = jnp.float32

G = 4
HG = 64 // G
W = 512
HL = 512 // G
TR = 2560
XW, ZW = 640, 640
PIECES = ((2 * XW, ZW, 0), (0, XW, 1), (XW, XW, 1), (2 * XW + ZW, ZW, 0))
STEP = 20
SKEW = 4
STAGES = 11, 17.5, 30.5


def split(x):
    hi = x.astype(BF)
    return hi, (x - hi.astype(F32)).astype(BF)


def product3(left, right_hi, right_lo):
    hi, lo = split(left)

    def dot(a, b):
        return lax.dot_general(a, b, (((1,), (1,)), ((), ())), preferred_element_type=F32)

    return dot(hi, right_hi) + (dot(hi, right_lo) + dot(lo, right_hi))


def kernel(
    incident_ref, d1_ref, c_ref, d2_ref, t1_ref, t2_ref, rhs_ref,
    solved_out, updated_out,
    x_ref, solved_ref, updated_ref,
    own_s, sib_s, own_t, sib_t, rhs,
    wh, wl, th, tl,
    xr, xt, x1b, x1s,
    part, got, summed, sol,
    upd, xa, xrel, za, zrel, zb, xb,
    loc, sib_tx, sib_rx, x_tx, x_rx, xg_tx, xg_rx, st_tx, st_rx, u_tx, u_rx, out_sem,
):
    r = lax.axis_index("rows")
    c = lax.axis_index("cols")
    y, xh = r // 2, r % 2
    q, k = c // 2, c % 2
    xl, z = q // 4, q % 4
    own_lanes = pl.ds(pl.multiple_of(k * 256, 256), 256)
    sib_lanes = pl.ds(pl.multiple_of((1 - k) * 256, 256), 256)
    sibling = (r, q * 2 + (1 - k))
    diagonal = r == q

    def send(src, dst, tx, rx, dev):
        pltpu.make_async_remote_copy(
            src_ref=src, dst_ref=dst, send_sem=tx, recv_sem=rx, device_id=dev, device_id_type=MESH
        ).start()

    def settle(ref, sem):
        pltpu.make_async_copy(ref, ref, sem).wait()

    first = pltpu.make_async_copy(incident_ref, x_ref, loc.at[6])
    first.start()
    own = [(d1_ref, own_s.at[0]), (c_ref, own_s.at[1]), (d2_ref, own_s.at[2]),
           (t1_ref, own_t.at[0]), (t2_ref, own_t.at[1]), (rhs_ref, rhs)]
    loads = [pltpu.make_async_copy(src, dst, loc.at[i]) for i, (src, dst) in enumerate(own)]
    for load in loads:
        load.start()

    barrier = pltpu.get_barrier_semaphore()
    plane = [(dq, dk) for dq in range(8) for dk in range(2) if (dq, dk) != (0, 0)]

    def plane_dev(dq, dk):
        return (r, ((q + dq) % 8) * 2 + (k + dk) % 2)

    def y_dev(d):
        return (((y + d) % 4) * 2 + xh, c)

    def greet(dev):
        pl.semaphore_signal(barrier, inc=1, device_id=dev, device_id_type=MESH)

    for dq, dk in plane:
        greet(plane_dev(dq, dk))
    for d in (1, 2, 3):
        greet(y_dev(d))
    for j in range(8):
        greet((q, j * 2 + (1 - k)))

        @pl.when(jnp.logical_not(jnp.logical_and(diagonal, j == q)))
        def _():
            greet((q, j * 2 + k))

    first.wait()
    per = 128 // HG
    place = lax.broadcasted_iota(jnp.int32, (32, 128), 1) // HG
    for core in range(2):
        for t in range(4):
            tile = None
            for j in range(per):
                chip = (t * per + j) % 8
                here = core * G + (t * per + j) // 8
                taken = x_ref[0, :, chip * 128 : chip * 128 + 128]
                shift = ((j - here) * HG) % 128
                if shift:
                    taken = pltpu.roll(taken, shift, 1)
                tile = taken if tile is None else jnp.where(place == j, taken, tile)
            xr[core, t] = tile.reshape(4, 8, 128)

    pl.semaphore_wait(barrier, 33 + jnp.where(diagonal, 0, 1))

    for dk in range(2):
        kk = (k + dk) % 2
        for jy in range(4):
            for jx in range(2):
                j = jy * 2 + jx
                src, dst = xr.at[kk, :, jy], xt.at[:, jy, c]
                if dk == 1:
                    send(src, dst, x_tx.at[0], x_rx.at[0], (j, r * 2 + kk))
                else:
                    me = jnp.logical_and(diagonal, r == j)

                    @pl.when(jnp.logical_not(me))
                    def _():
                        send(src, dst, x_tx.at[0], x_rx.at[0], (j, r * 2 + kk))

                    @pl.when(me)
                    def _():
                        pltpu.make_async_copy(src, dst, x_rx.at[0]).start()

    small = [d1_ref, c_ref, d2_ref]
    send(small[0], sib_s.at[0], sib_tx.at[0], sib_rx.at[0], sibling)

    def ready_small(i):
        loads[i].wait()
        wh[i, :, own_lanes], wl[i, :, own_lanes] = split(own_s[i])
        settle(sib_s.at[i], sib_rx.at[i])
        wh[i, :, sib_lanes], wl[i, :, sib_lanes] = split(sib_s[i])

    def ready_trail(i):
        loads[3 + i].wait()
        settle(sib_t.at[i], sib_rx.at[3 + i])

        @pl.loop(0, 20)
        def _(n):
            rows = pl.ds(pl.multiple_of(n * 128, 128), 128)
            th[i, rows, own_lanes], tl[i, rows, own_lanes] = split(own_t[i, rows, :])
            th[i, rows, sib_lanes], tl[i, rows, sib_lanes] = split(sib_t[i, rows, :])

    ready_small(0)
    settle(xt.at[:, y], x_rx.at[0])
    for g in range(G):
        for d in (1, 2, 3):
            block = xt.at[g, y]
            send(block, block, xg_tx.at[g], xg_rx.at[g], y_dev(d))
    send(small[1], sib_s.at[1], sib_tx.at[1], sib_rx.at[1], sibling)
    for dq, dk in plane:
        lanes = pl.ds(pl.multiple_of(((q + dq) % 8) * 128, 128), 128)
        send(x_ref.at[1, :, lanes], x1b.at[c], x_tx.at[1], x_rx.at[1], plane_dev(dq, dk))
    x1b[c] = x_ref[1, :, pl.ds(pl.multiple_of(q * 128, 128), 128)]
    send(small[2], sib_s.at[2], sib_tx.at[2], sib_rx.at[2], sibling)
    for i, t_ref in enumerate((t1_ref, t2_ref)):
        send(t_ref, sib_t.at[i], sib_tx.at[3 + i], sib_rx.at[3 + i], sibling)

    def three_pieces(s, g):
        return sol.at[s, g, pl.ds(0, 3)]

    def solved_of(s, g):
        return jnp.concatenate([sol[s, g, piece].reshape(8 * HG, 128) for piece in range(4)], axis=1)

    def multiply(s, g):
        if s == 0:
            settle(xt.at[g, pl.ds(0, 3)], xg_rx.at[g])
            left = jnp.concatenate([xt[g, :, held].reshape(32, HL) for held in range(16)], axis=0).T
        else:
            settle(three_pieces(s - 1, g), st_rx.at[2, s - 1, g])
            left = solved_of(s - 1, g)
        out = product3(left, wh[s], wl[s])
        part[s, g] = out.reshape(8, HG, W)
        for d in range(1, 8):
            to = (q + d) % 8
            send(part.at[s, g, to], got.at[s, g, d - 1], st_tx.at[0, s, g], st_rx.at[0, s, g], (r, to * 2 + k))

    def sum_up(s, g):
        settle(got.at[s, g], st_rx.at[0, s, g])
        total = part[s, g, q]
        for d in range(7):
            total = total + got[s, g, d]
        rows = pl.ds(g * HG, HG)
        if s == 1:
            total = x1s[k, rows] - total
        else:
            solved_ref[s // 2, rows] = total
            pltpu.make_async_copy(solved_ref.at[s // 2, rows], solved_out.at[s // 2, rows], out_sem.at[s // 2, g]).start()
        for piece in range(4):
            summed[s, g, piece] = total[:, piece * 128 : piece * 128 + 128]
        for jy in range(4):
            for jx in range(2):
                j = jy * 2 + jx
                src, dst = summed.at[s, g, jy], sol.at[s, g, jy, q]
                me = jnp.logical_and(diagonal, r == j)

                @pl.when(jnp.logical_not(me))
                def _():
                    send(src, dst, st_tx.at[1, s, g], st_rx.at[1, s, g], (j, r * 2 + k))

                @pl.when(me)
                def _():
                    pltpu.make_async_copy(src, dst, st_rx.at[1, s, g]).start()

    def spread(s, g):
        block = sol.at[s, g, y]
        settle(block, st_rx.at[1, s, g])
        for d in (1, 2, 3):
            send(block, block, st_tx.at[2, s, g], st_rx.at[2, s, g], y_dev(d))

    def ready_second():
        settle(x1b.at[pl.ds(0, 15)], x_rx.at[1])
        x1s[...] = x1b[...].reshape(512, 128).T.reshape(2, 64, W)

    def first_trail(pair, p):
        start, width, _ = PIECES[p]
        columns = slice(start, start + width)
        both = slice(2 * pair, 2 * pair + 2)
        left = jnp.concatenate([solved_of(0, 2 * pair), solved_of(0, 2 * pair + 1)], axis=0)
        upd[both, :, :, columns] = product3(left, th[0, columns], tl[0, columns]).reshape(2, 8, HG, width)

    across = (r, ((1 - xl) * 4 + z) * 2 + k)

    def z_dev(d):
        return (r, (xl * 4 + (z + d) % 4) * 2 + k)

    ways = (1, 3)
    sides = ((z + 1) % 4, (z + 3) % 4)
    opposite = (z + 2) % 4

    def second_trail(g):
        settle(three_pieces(2, g), st_rx.at[2, 2, g])
        left = solved_of(2, g)
        for p, (start, width, x_first) in enumerate(PIECES):
            columns = slice(start, start + width)
            upd[g, :, :, columns] += product3(left, th[1, columns], tl[1, columns]).reshape(8, HG, width)
            lanes = pl.ds(start, width)
            if x_first:
                send(upd.at[g, pl.ds((1 - xl) * 4, 4), :, lanes], xa.at[g, p - 1], u_tx.at[0, g, p], u_rx.at[0, g, p], across)
            else:
                n = p // 3
                for x in range(2):
                    send(upd.at[g, x * 4 + opposite, :, lanes], zrel.at[g, n, x], u_tx.at[0, g, p], u_rx.at[0, g, p], z_dev(ways[x]))
                for x in range(2):
                    send(upd.at[g, (1 - x) * 4 + sides[x], :, lanes], zb.at[g, n, x, 1 - x],
                         u_tx.at[1, g, p], u_rx.at[1, g, p], z_dev(ways[x]))

    def middle(g):
        for p, (start, width, x_first) in enumerate(PIECES):
            columns = slice(start, start + width)
            lanes = pl.ds(start, width)
            if x_first:
                settle(xa.at[g, p - 1], u_rx.at[0, g, p])
                upd[g, pl.ds(xl * 4, 4), :, columns] += xa[g, p - 1]
                for h in range(2):
                    rows = pl.ds(h * (HG // 2), HG // 2)
                    send(upd.at[g, xl * 4 + opposite, rows, lanes], xrel.at[g, p - 1, h],
                         u_tx.at[1, g, p], u_rx.at[1, g, p], z_dev(ways[h]))
                for h in range(2):
                    rows = pl.ds((1 - h) * (HG // 2), HG // 2)
                    send(upd.at[g, xl * 4 + sides[h], rows, lanes], za.at[g, p - 1, h, rows],
                         u_tx.at[2, g, p], u_rx.at[2, g, p], z_dev(ways[h]))
            else:
                n = p // 3
                settle(zrel.at[g, n], u_rx.at[0, g, p])
                for x in range(2):
                    upd[g, x * 4 + sides[x], :, columns] += zrel[g, n, x]
                    send(upd.at[g, x * 4 + sides[x], :, lanes], zb.at[g, n, x, x], u_tx.at[1, g, p], u_rx.at[1, g, p], z_dev(ways[x]))

    def later(g):
        for p, (start, width, x_first) in enumerate(PIECES):
            columns = slice(start, start + width)
            lanes = pl.ds(start, width)
            if x_first:
                settle(xrel.at[g, p - 1], u_rx.at[1, g, p])
                for h in range(2):
                    half = slice(h * (HG // 2), (h + 1) * (HG // 2))
                    rows = pl.ds(h * (HG // 2), HG // 2)
                    upd[g, xl * 4 + sides[h], half, columns] += xrel[g, p - 1, h]
                    send(upd.at[g, xl * 4 + sides[h], rows, lanes], za.at[g, p - 1, h, rows],
                         u_tx.at[2, g, p], u_rx.at[2, g, p], z_dev(ways[h]))
            else:
                n = p // 3
                settle(zb.at[g, n], u_rx.at[1, g, p])
                for x in range(2):
                    upd[g, x * 4 + z, :, columns] += zb[g, n, 0, x] + zb[g, n, 1, x]
                send(upd.at[g, (1 - xl) * 4 + z, :, lanes], xb.at[g, n], u_tx.at[2, g, p], u_rx.at[2, g, p], across)

    def finish(g):
        rows = pl.ds(g * HG, HG)
        for p, (start, width, x_first) in enumerate(PIECES):
            columns = slice(start, start + width)
            total = upd[g, q, :, columns]
            if x_first:
                settle(za.at[g, p - 1], u_rx.at[2, g, p])
                total = total + (za[g, p - 1, 0] + za[g, p - 1, 1])
            else:
                settle(xb.at[g, p // 3], u_rx.at[2, g, p])
                total = total + xb[g, p // 3]
            updated_ref[rows, columns] = rhs[rows, columns] - total
        pltpu.make_async_copy(updated_ref.at[rows], updated_out.at[rows], out_sem.at[2, g]).start()

    order = []
    for g in range(G):
        for s in range(3):
            begin = s * STEP + g * SKEW
            order += [(begin, multiply, (s, g)), (begin + 6.4, sum_up, (s, g)), (begin + 12.4, spread, (s, g))]
        begin = 3 * STEP + g * SKEW
        order += [(begin, second_trail, (g,)), (begin + STAGES[0], middle, (g,)),
                  (begin + STAGES[1], later, (g,)), (begin + STAGES[2], finish, (g,))]
    order += [(0.1, ready_small, (1,)), (0.2, ready_small, (2,)), (4.4, ready_trail, (0,)), (8.4, ready_second, ()),
              (12.4, ready_trail, (1,)), (3 * STEP - 0.4, loads[5].wait, ())]
    for pair in range(2):
        order += [(STEP + (2 * pair + 1) * SKEW + 0.4 + 2 * p, first_trail, (pair, p)) for p in range(4)]
    for _, work, which in sorted(order, key=lambda entry: entry[0]):
        work(*which)

    for i in range(3):
        settle(sib_s.at[i], sib_tx.at[i])
    for i in range(2):
        settle(sib_t.at[i], sib_tx.at[3 + i])

    @pl.when(diagonal)
    def _():
        settle(xt.at[:, 0, pl.ds(0, 15)], x_tx.at[0])

    @pl.when(jnp.logical_not(diagonal))
    def _():
        settle(xt.at[:, 0], x_tx.at[0])

    settle(x1b.at[pl.ds(0, 15)], x_tx.at[1])
    for g in range(G):
        rows = pl.ds(g * HG, HG)
        settle(solved_ref.at[0, rows], out_sem.at[0, g])
        settle(solved_ref.at[1, rows], out_sem.at[1, g])
        settle(updated_ref.at[rows], out_sem.at[2, g])
        settle(xt.at[g, pl.ds(0, 3)], xg_tx.at[g])
        for s in range(3):
            settle(got.at[s, g], st_tx.at[0, s, g])

            @pl.when(diagonal)
            def _():
                settle(sol.at[s, g, 0, pl.ds(0, 7)], st_tx.at[1, s, g])

            @pl.when(jnp.logical_not(diagonal))
            def _():
                settle(sol.at[s, g, 0], st_tx.at[1, s, g])

            settle(three_pieces(s, g), st_tx.at[2, s, g])
        for p, (_, _, x_first) in enumerate(PIECES):
            if x_first:
                settle(xa.at[g, p - 1], u_tx.at[0, g, p])
                settle(xrel.at[g, p - 1], u_tx.at[1, g, p])
                settle(za.at[g, p - 1], u_tx.at[2, g, p])
            else:
                settle(zrel.at[g, p // 3], u_tx.at[0, g, p])
                settle(zb.at[g, p // 3], u_tx.at[1, g, p])
                settle(xb.at[g, p // 3], u_tx.at[2, g, p])


def hand_over(solved_in, updated_in, solved_out, updated_out, sems):
    copies = [
        pltpu.make_async_copy(solved_in, solved_out, sems.at[0]),
        pltpu.make_async_copy(updated_in, updated_out, sems.at[1]),
    ]
    for copy in copies:
        copy.start()
    for copy in copies:
        copy.wait()


def on_device(incident, diag_first, coupling, diag_second, trail_first, trail_second, trail_rhs):
    far = pl.BlockSpec(memory_space=pl.ANY)
    dma = pltpu.SemaphoreType.DMA
    shapes = (jax.ShapeDtypeStruct((2, 64, W), F32), jax.ShapeDtypeStruct((64, TR), F32))
    results = pl.pallas_call(
        kernel,
        out_shape=shapes,
        in_specs=[far] * 7,
        out_specs=(far, far),
        scratch_shapes=[
            pltpu.VMEM((2, 32, 1024), F32),
            pltpu.VMEM((2, 64, W), F32),
            pltpu.VMEM((64, TR), F32),
            pltpu.VMEM((3, W, 256), F32),
            pltpu.VMEM((3, W, 256), F32),
            pltpu.VMEM((2, TR, 256), F32),
            pltpu.VMEM((2, TR, 256), F32),
            pltpu.VMEM((64, TR), F32),
            pltpu.VMEM((3, W, W), BF),
            pltpu.VMEM((3, W, W), BF),
            pltpu.VMEM((2, TR, W), BF),
            pltpu.VMEM((2, TR, W), BF),
            pltpu.VMEM((2, G, 4, 8, HL), F32),
            pltpu.VMEM((G, 4, 16, 8, HL), F32),
            pltpu.VMEM((16, 32, 128), F32),
            pltpu.VMEM((2, 64, W), F32),
            pltpu.VMEM((3, G, 8, HG, W), F32),
            pltpu.VMEM((3, G, 7, HG, W), F32),
            pltpu.VMEM((3, G, 4, HG, 128), F32),
            pltpu.VMEM((3, G, 4, 8, HG, 128), F32),
            pltpu.VMEM((G, 8, HG, TR), F32),
            pltpu.VMEM((G, 2, 4, HG, XW), F32),
            pltpu.VMEM((G, 2, 2, HG // 2, XW), F32),
            pltpu.VMEM((G, 2, 2, HG, XW), F32),
            pltpu.VMEM((G, 2, 2, HG, ZW), F32),
            pltpu.VMEM((G, 2, 2, 2, HG, ZW), F32),
            pltpu.VMEM((G, 2, HG, ZW), F32),
            dma((7,)), dma((5,)), dma((5,)), dma((2,)), dma((2,)), dma((G,)), dma((G,)),
            dma((3, 3, G)), dma((3, 3, G)), dma((3, G, 4)), dma((3, G, 4)), dma((3, G)),
        ],
        compiler_params=pltpu.CompilerParams(
            collective_id=0, has_side_effects=True, vmem_limit_bytes=60 * 1024 * 1024
        ),
        name="solve",
    )(jnp.swapaxes(incident, 1, 2), diag_first, coupling, diag_second, trail_first, trail_second, trail_rhs)
    return pl.pallas_call(
        hand_over,
        out_shape=shapes,
        in_specs=[pl.BlockSpec(memory_space=pltpu.VMEM)] * 2,
        out_specs=(far, far),
        scratch_shapes=[dma((2,))],
        name="hand_over",
    )(*results)


def solution(mesh):
    split_all = P("rows", "cols")
    return jax.shard_map(
        on_device,
        mesh=mesh,
        in_specs=(P(None, None, ("rows", "cols")),) + (split_all,) * 5 + (P("cols", "rows"),),
        out_specs=(P(None, "cols", "rows"), P("cols", "rows")),
        check_vma=False,
    )
```
